32 devices in a mesh: groups: 2 (over y), dp: 4 (over z), tensor: 4 (over x, core).
Axes of the slice: x: 2, y: 2, z: 4, core: 2. Of those that a mesh axis runs over, the one named last changes fastest.
Arguments:
- tokens: bfloat16 [1024, 16384], P(('groups', 'dp')), parts along dimension 0, may hold values from -6 to 6
- gate_weight: bfloat16 [16384, 512], P('dp', 'tensor'), may hold values from -0.046875 to 0.046875
- up_weight: bfloat16 [16384, 512], P('dp', 'tensor'), may hold values from -0.046875 to 0.046875
- down_weight: bfloat16 [512, 16384], P('tensor', 'dp'), may hold values from -0.5 to 0.5
- gate_mask: int32 [128, 4], P(None, 'tensor'), may hold values from 0 to 1, as said below
- up_mask: int32 [128, 4], P(None, 'tensor'), may hold values from 0 to 1, as said below
- down_mask: int32 [4, 128], P('tensor'), may hold values from 0 to 1, as said below
Outputs:
- mixed: bfloat16 [1024, 16384], P(('groups', 'dp'), 'tensor'), parts along dimension 0
The draws below stay inside these ranges and needn't reach their ends.
There are 2 independent parts, one for each index of `groups`. The reference program is written for one: setup_inputs(seed, part) draws one part's arguments, and reference() takes and returns one part's arrays. A program takes and returns all parts, laid end to end along the dimension named above; an argument that names none is the same for every part. Nothing has to cross between parts.
Inputs may be any that keep to these rules, and one draw needn't show every extreme that they name: `gate_mask`: each block flag; every shard of a mask that one device holds for the layer's weights (32 blocks: rows of one dp index and hidden units of one tensor index) keeps between 8 and 24 blocks, and some such shard keeps exactly 24 in every draw. `up_mask`: as for gate_mask, drawn apart. `down_mask`: as for gate_mask, for the down projection's shards (1 hidden blocks of one tensor index times 32 width blocks of one dp index).
All inputs are finite; a program needn't handle non-finite values.
Results may differ from the reference program's by a relative error of at most 0.006.
Values may be sent and summed in bfloat16 or wider, within the bound.
A program may use at most 64 MiB of HBM per device.

```python
import jax
import jax.numpy as jnp
from jax import lax

D = 16384
BS = 128
HB = 1
FF = 512
TOKENS = 512
RB = 32
CAP = 24
N_DP = 4
N_TENSOR = 4


def shard_flags(key, shards, blocks, capacity):
    count_key, perm_key, full_key = jax.random.split(key, 3)
    counts = jax.random.randint(count_key, (shards,), blocks // 4, capacity + 1)
    fullest = jax.random.randint(full_key, (), 0, shards)
    counts = jnp.where(jnp.arange(shards) == fullest, capacity, counts)
    ranking = jax.vmap(lambda subkey: jax.random.permutation(subkey, blocks))(jax.random.split(perm_key, shards))
    return (ranking < counts[:, None]).astype(jnp.int32)


def width_side(key):
    keep_flags = shard_flags(key, N_DP * N_TENSOR, RB * HB, CAP)
    keep_flags = keep_flags.reshape(N_DP, N_TENSOR, RB, HB).transpose(0, 2, 1, 3)
    return keep_flags.reshape(N_DP * RB, N_TENSOR * HB)


def draw_gate_mask(key, part):
    key = jax.random.fold_in(key, 11)
    return width_side(key)


def draw_up_mask(key, part):
    key = jax.random.fold_in(key, 23)
    return width_side(key)


def draw_down_mask(key, part):
    key = jax.random.fold_in(key, 37)
    keep_flags = shard_flags(key, N_TENSOR * N_DP, HB * RB, CAP)
    keep_flags = keep_flags.reshape(N_TENSOR, N_DP, HB, RB).transpose(0, 2, 1, 3)
    return keep_flags.reshape(N_TENSOR * HB, N_DP * RB)


def level_of(rng, dims, pieces, low, high):
    factor_of, own = 1.0, jax.random.fold_in(rng, 6)
    for position, parts in pieces:
        draws = jnp.exp(jax.random.uniform(jax.random.fold_in(own, position), (parts,), jnp.float32, low / len(pieces), high / len(pieces)))
        factor_of = factor_of * jnp.repeat(draws, dims[position] // parts).reshape([-1 if axis == position else 1 for axis in range(len(dims))])
    return factor_of


def bell_draw(stream_key, dims, scale, bound, pieces=(), kind=jnp.bfloat16):
    loudness = level_of(stream_key, dims, pieces, -0.22, 0.18) if pieces else 1.0
    values = jax.random.normal(stream_key, dims, jnp.float32) * scale * loudness
    return jnp.minimum(jnp.maximum(values, -bound), bound).astype(kind)


def setup_inputs(seed: int = 0, part: int = 0) -> dict:
    streams_of = jax.random.split(jax.random.key(seed), 8)
    own_keys = jax.random.split(jax.random.fold_in(streams_of[7], part), 8)
    return {
        "tokens": bell_draw(own_keys[0], (TOKENS, D), 1.0, 6.0, ((0, 4),)),
        "gate_weight": bell_draw(streams_of[1], (D, FF), D ** -0.5, 0.046875, ((0, 4), (1, 4))),
        "up_weight": bell_draw(streams_of[2], (D, FF), D ** -0.5, 0.046875, ((0, 4), (1, 4))),
        "down_weight": bell_draw(streams_of[3], (FF, D), (FF // 4) ** -0.5, 0.5, ((0, 4), (1, 4))),
        "gate_mask": draw_gate_mask(jax.random.fold_in(streams_of[7], 71), part),
        "up_mask": draw_up_mask(jax.random.fold_in(streams_of[7], 71), part),
        "down_mask": draw_down_mask(jax.random.fold_in(streams_of[7], 71), part),
    }


def expand_mask(mask):
    return jnp.repeat(jnp.repeat(mask, BS, axis=0), BS, axis=1).astype(jnp.bfloat16)


def reference(tokens, gate_weight, up_weight, down_weight, gate_mask, up_mask, down_mask):
    gate_sum = jnp.dot(tokens, gate_weight * expand_mask(gate_mask), preferred_element_type=jnp.float32)
    up_sum = jnp.dot(tokens, up_weight * expand_mask(up_mask), preferred_element_type=jnp.float32)
    hidden = (jax.nn.silu(gate_sum) * up_sum).astype(jnp.bfloat16)
    down_pruned = down_weight * expand_mask(down_mask)
    hid_share = FF // N_TENSOR

    def add_share(running, shard_index):
        first = (shard_index * hid_share).astype(jnp.int32)
        hid_cols = lax.dynamic_slice_in_dim(hidden, first, hid_share, 1)
        down_rows = lax.dynamic_slice_in_dim(down_pruned, first, hid_share, 0)
        rounded = jnp.dot(hid_cols, down_rows, preferred_element_type=jnp.float32).astype(jnp.bfloat16)
        rounded = lax.optimization_barrier(rounded)
        return running + rounded.astype(jnp.float32), None

    running, unused = lax.scan(add_share, jnp.zeros((TOKENS, D), jnp.float32), jnp.arange(N_TENSOR, dtype=jnp.int32))
    return running.astype(jnp.bfloat16)
```

```python
import functools

import jax
import jax.numpy as jnp
from jax import lax
from jax.experimental import pallas as pl
from jax.experimental.pallas import tpu as pltpu
from jax.sharding import PartitionSpec as P

BS = 128
MESH = pl.DeviceIdType.MESH
CHUNKS = 4


def expand_mask(mask):
    return jnp.repeat(jnp.repeat(mask, BS, axis=0), BS, axis=1).astype(jnp.bfloat16)


def gathered(tokens, gate_weight, up_weight, down_weight, gate_mask, up_mask, down_mask):
    dp_index = lax.axis_index("dp")
    row_blocks = gate_weight.shape[0] // BS
    row_start = dp_index * row_blocks
    gate_pruned = gate_weight * expand_mask(
        lax.dynamic_slice_in_dim(gate_mask, row_start, row_blocks, 0)
    )
    up_pruned = up_weight * expand_mask(lax.dynamic_slice_in_dim(up_mask, row_start, row_blocks, 0))
    gate_part = jnp.dot(
        tokens,
        lax.all_gather(gate_pruned, "dp", axis=0, tiled=True),
        preferred_element_type=jnp.float32,
    )
    up_part = jnp.dot(
        tokens,
        lax.all_gather(up_pruned, "dp", axis=0, tiled=True),
        preferred_element_type=jnp.float32,
    )
    hidden = (jax.nn.silu(gate_part) * up_part).astype(jnp.bfloat16)
    down_pruned = down_weight * expand_mask(
        lax.dynamic_slice_in_dim(down_mask, row_start, row_blocks, 1)
    )
    partial_out = jnp.dot(
        hidden,
        lax.all_gather(down_pruned, "dp", axis=1, tiled=True),
        preferred_element_type=jnp.float32,
    )
    return lax.psum_scatter(
        partial_out.astype(jnp.bfloat16), "tensor", scatter_dimension=1, tiled=True
    )


def kernel(n, tok_hbm, gate_hbm, up_hbm, down_hbm, gmask, umask, dmask, out,
           T, W, PC, G, psend, precv, H,
           ch_s, ch_r, ip_s, ip_r, y_s, y_r, tz_s, tz_r, tx_s, tx_r, tc_s, tc_r,
           p_s, p_r, h_s, h_r, ld):
    g = lax.axis_index("groups")
    z = lax.axis_index("dp")
    t = lax.axis_index("tensor")
    rows = tok_hbm.shape[0]
    width = gate_hbm.shape[0]
    hid = gate_hbm.shape[1]
    half = hid // 2
    quarter = rows // n
    cw = width // CHUNKS
    blocks = width // BS
    zero = jnp.int32(0)
    t_core = jnp.where(lax.rem(t, 2) == zero, t + 1, t - 1)
    t_x = lax.rem(t + 2, n)

    def mod(a):
        return lax.rem(a + 2 * n, n)

    def remote(src, dst, ss, rs, **where):
        return pltpu.make_async_remote_copy(
            src_ref=src, dst_ref=dst, send_sem=ss, recv_sem=rs, device_id=where,
            device_id_type=MESH)

    own_cols = pl.ds(pl.multiple_of(z * width, 128), width)
    load_down = pltpu.make_async_copy(
        down_hbm.at[pl.ds(pl.multiple_of(g * half, half), half), :], PC.at[z], ld.at[0])
    load_tok = pltpu.make_async_copy(
        tok_hbm.at[:, own_cols], T.at[pl.ds(pl.multiple_of(z * rows, rows), rows), :], ld.at[1])
    load_gate = pltpu.make_async_copy(gate_hbm, W.at[:, pl.ds(0, hid)], ld.at[2])
    load_up = pltpu.make_async_copy(up_hbm, W.at[:, pl.ds(hid, hid)], ld.at[3])
    load_down.start()

    barrier = pltpu.get_barrier_semaphore()
    for d in range(1, n):
        pl.semaphore_signal(barrier, inc=1, device_id={"dp": mod(z + d)}, device_id_type=MESH)
        pl.semaphore_signal(barrier, inc=1, device_id={"tensor": mod(t + d)}, device_id_type=MESH)
    pl.semaphore_signal(barrier, inc=1, device_id={"groups": 1 - g}, device_id_type=MESH)
    load_gate.start()
    load_up.start()
    load_tok.start()

    load_down.wait()
    for b in range(blocks):
        keep = dmask[z * blocks + b].astype(jnp.float32)
        cols = pl.ds(b * BS, BS)
        PC[z, :, cols] = (PC[z, :, cols].astype(jnp.float32) * keep).astype(jnp.bfloat16)
    pl.semaphore_wait(barrier, 2 * (n - 1) + 1)

    pending = []

    def go(copy, cond=None):
        pending.append((copy, cond))
        if cond is None:
            copy.start()
        else:
            pl.when(cond)(copy.start)

    def chunk(c):
        return pl.ds(c * cw, cw)

    def g_rows(ts, h):
        return pl.ds(pl.multiple_of(ts * hid + h * half, half), half)

    def chain(direction, r, c):
        k = z - r if direction == 0 else z + r
        to = z + 1 if direction == 0 else z - 1
        ok = (k >= 0) & (to < n) if direction == 0 else (k < n) & (to >= 0)
        kk = mod(k)
        return remote(
            PC.at[kk, :, chunk(c)], PC.at[kk, :, chunk(c)], ch_s.at[direction, r, c],
            ch_r.at[direction, r, c], dp=mod(to)), ok

    def dispatch(k, slot, c, ok):
        copy = remote(
            PC.at[k, :, chunk(c)], G.at[g_rows(t, g), chunk(c)], ip_s.at[slot, c],
            ip_r.at[t, c], tensor=k)
        go(copy, ok & (k != t))

    def across(e, c):
        ts = mod(t + e)
        ref = G.at[g_rows(ts, g), chunk(c)]
        return remote(ref, ref, y_s.at[e, c], y_r.at[e, c], groups=1 - g)

    def arrived(e, c):
        ts = mod(t + e)
        ref = G.at[g_rows(ts, g), chunk(c)]
        return remote(ref, ref, ip_s.at[0, c], ip_r.at[ts, c], tensor=ts)

    crossings = [[across(e, c) for e in range(n)] for c in range(CHUNKS)]

    def owner_round(r):
        @pl.when(jnp.abs(z - t) == r)
        def _():
            for c in range(CHUNKS):
                G[g_rows(t, g), chunk(c)] = PC[t, :, chunk(c)]
                crossings[c][0].start()
                for e in range(1, n):
                    arrived(e, c).wait_recv()
                    crossings[c][e].start()

    for c in range(CHUNKS):
        for direction in range(2):
            copy, ok = chain(direction, 0, c)
            go(copy, ok)
    for c in range(CHUNKS):
        dispatch(z, 0, c, True)

    def token_piece(s, q):
        return T.at[pl.ds(pl.multiple_of(s * rows + q * quarter, quarter), quarter), :]

    for d in (2, 1, 3):
        k = mod(z + d)
        go(remote(
            tok_hbm.at[pl.ds(pl.multiple_of(t * quarter, quarter), quarter),
                       pl.ds(pl.multiple_of(k * width, 128), width)],
            token_piece(z, t), tz_s.at[d - 1], tz_r.at[d - 1], dp=k))

    def relay_tokens(d):
        s = mod(z - d)
        mine = token_piece(s, t)
        remote(mine, mine, tz_s.at[d - 1], tz_r.at[d - 1], dp=s).wait_recv()
        go(remote(mine, mine, tx_s.at[d - 1], tx_r.at[d - 1], tensor=t_x))
        go(remote(mine, mine, tc_s.at[0, d - 1], tc_r.at[0, d - 1], tensor=t_core))

    def relay_x(d):
        s = mod(z - d)
        other = token_piece(s, t_x)
        remote(other, other, tx_s.at[d - 1], tx_r.at[d - 1], tensor=t_x).wait_recv()
        go(remote(other, other, tc_s.at[1, d - 1], tc_r.at[1, d - 1], tensor=t_core))

    def products(s):
        return jnp.dot(
            T[pl.ds(pl.multiple_of(s * rows, rows), rows), :], W[...],
            preferred_element_type=jnp.float32)

    def finish_tokens(d):
        s = mod(z - d)
        for hop, q in enumerate((t_core, lax.rem(t_core + 2, n))):
            piece = token_piece(s, q)
            remote(piece, piece, tc_s.at[hop, d - 1], tc_r.at[hop, d - 1],
                   tensor=t_core).wait_recv()
        psend[d - 1] = products(s).astype(jnp.bfloat16)
        go(remote(psend.at[d - 1], precv.at[d - 1], p_s.at[d - 1], p_r.at[d - 1], dp=s))

    load_gate.wait()
    load_up.wait()

    @pl.loop(0, blocks)
    def _(b):
        at = pl.ds(pl.multiple_of(b * BS, BS), BS)
        gk = gmask[z * blocks + b].astype(jnp.float32)
        uk = umask[z * blocks + b].astype(jnp.float32)
        W[at, pl.ds(0, hid)] = (W[at, pl.ds(0, hid)].astype(jnp.float32) * gk).astype(jnp.bfloat16)
        W[at, pl.ds(hid, hid)] = (W[at, pl.ds(hid, hid)].astype(jnp.float32) * uk).astype(jnp.bfloat16)

    load_tok.wait()
    own = products(z)
    owner_round(0)

    for r in range(1, n):
        for c in range(CHUNKS):
            for direction in range(2):
                k = z - r if direction == 0 else z + r
                ok = k >= 0 if direction == 0 else k < n
                kk = mod(k)
                piece = PC.at[kk, :, chunk(c)]
                came = remote(piece, piece, ch_s.at[direction, r - 1, c],
                              ch_r.at[direction, r - 1, c], dp=mod(z + 1))
                pl.when(ok)(came.wait_recv)
                if r < n - 1:
                    copy, also = chain(direction, r, c)
                    go(copy, ok & also)
                dispatch(kk, 2 * r - 1 + direction, c, ok)
        owner_round(r)
        relay_tokens((1, 3, 2)[r - 1])
    for d in (1, 3, 2):
        relay_x(d)
    for d in (1, 3, 2):
        finish_tokens(d)

    total = own
    for d in range(1, n):
        ref = precv.at[d - 1]
        remote(ref, ref, p_s.at[d - 1], p_r.at[d - 1], dp=mod(z + d)).wait_recv()
        total = total + precv[d - 1].astype(jnp.float32)
    gate, up = total[:, :hid], total[:, hid:]
    mine = pl.ds(pl.multiple_of(t * hid, hid), hid)
    H[:, mine] = (gate / (1.0 + jnp.exp(-gate)) * up).astype(jnp.bfloat16)
    for d in range(1, n):
        go(remote(H.at[:, mine], H.at[:, mine], h_s.at[d - 1], h_r.at[d - 1], tensor=mod(t + d)))
    for d in range(1, n):
        theirs = H.at[:, pl.ds(pl.multiple_of(mod(t - d) * hid, hid), hid)]
        remote(theirs, theirs, h_s.at[d - 1], h_r.at[d - 1], tensor=mod(t + d)).wait_recv()

    for c in range(CHUNKS):
        for e in range(n):
            ts = mod(t + e)
            ref = G.at[g_rows(ts, 1 - g), chunk(c)]
            remote(ref, ref, y_s.at[e, c], y_r.at[e, c], groups=1 - g).wait_recv()
        out[:, chunk(c)] = jnp.dot(
            H[...], G[:, chunk(c)], preferred_element_type=jnp.float32).astype(jnp.bfloat16)

    for copy, cond in pending:
        if cond is None:
            copy.wait_send()
        else:
            pl.when(cond)(copy.wait_send)
    for row in crossings:
        for copy in row:
            copy.wait_send()


def fused(n, tokens, gate_weight, up_weight, down_weight, gate_mask, up_mask, down_mask):
    rows = tokens.shape[0]
    width, hid = gate_weight.shape
    bf16 = jnp.bfloat16
    dma = pltpu.SemaphoreType.DMA
    anyspec = pl.BlockSpec(memory_space=pl.ANY)
    smem = pl.BlockSpec(memory_space=pltpu.SMEM)
    return pl.pallas_call(
        functools.partial(kernel, n),
        out_shape=jax.ShapeDtypeStruct((rows, width), bf16),
        in_specs=[anyspec] * 4 + [smem] * 3,
        out_specs=pl.BlockSpec(memory_space=pltpu.VMEM),
        scratch_shapes=[
            pltpu.VMEM((n * rows, width), bf16),
            pltpu.VMEM((width, 2 * hid), bf16),
            pltpu.VMEM((n, hid // 2, width), bf16),
            pltpu.VMEM((n * hid, width), bf16),
            pltpu.VMEM((n - 1, rows, 2 * hid), bf16),
            pltpu.VMEM((n - 1, rows, 2 * hid), bf16),
            pltpu.VMEM((rows, n * hid), bf16),
            dma((2, n - 1, CHUNKS)), dma((2, n - 1, CHUNKS)),
            dma((2 * n - 1, CHUNKS)), dma((n, CHUNKS)),
            dma((n, CHUNKS)), dma((n, CHUNKS)),
            dma((n - 1,)), dma((n - 1,)),
            dma((n - 1,)), dma((n - 1,)),
            dma((2, n - 1)), dma((2, n - 1)),
            dma((n - 1,)), dma((n - 1,)),
            dma((n - 1,)), dma((n - 1,)),
            dma((4,)),
        ],
        compiler_params=pltpu.CompilerParams(
            collective_id=0, has_side_effects=True, vmem_limit_bytes=40 * 1024 * 1024),
        cost_estimate=pl.CostEstimate(
            flops=2 * rows * n * width * 3 * hid, bytes_accessed=16 * 1024 * 1024,
            transcendentals=rows * hid),
    )(tokens, gate_weight, up_weight, down_weight, gate_mask.reshape(-1), up_mask.reshape(-1),
      down_mask.reshape(-1))


def solution(mesh):
    n_dp, n_tensor, n_groups = mesh.shape["dp"], mesh.shape["tensor"], mesh.shape["groups"]
    placed = (
        P(("groups", "dp"), None),
        P("dp", "tensor"),
        P("dp", "tensor"),
        P("tensor", "dp"),
        P(None, "tensor"),
        P(None, "tensor"),
        P("tensor", None),
    )
    body = gathered
    if n_dp == 4 and n_tensor == 4 and n_groups == 2:
        body = functools.partial(fused, n_dp)
    return jax.shard_map(
        body, mesh=mesh, in_specs=placed, out_specs=P(("groups", "dp"), "tensor"), check_vma=False
    )
```

```python
import functools

import jax
import jax.numpy as jnp
from jax import lax
from jax.experimental import pallas as pl
from jax.experimental.pallas import tpu as pltpu
from jax.sharding import PartitionSpec as P

BS = 128
MESH = pl.DeviceIdType.MESH
CHUNKS = 4


def expand_mask(mask):
    return jnp.repeat(jnp.repeat(mask, BS, axis=0), BS, axis=1).astype(jnp.bfloat16)


def gathered(tokens, gate_weight, up_weight, down_weight, gate_mask, up_mask, down_mask):
    dp_index = lax.axis_index("dp")
    row_blocks = gate_weight.shape[0] // BS
    row_start = dp_index * row_blocks
    gate_pruned = gate_weight * expand_mask(
        lax.dynamic_slice_in_dim(gate_mask, row_start, row_blocks, 0)
    )
    up_pruned = up_weight * expand_mask(lax.dynamic_slice_in_dim(up_mask, row_start, row_blocks, 0))
    gate_part = jnp.dot(
        tokens,
        lax.all_gather(gate_pruned, "dp", axis=0, tiled=True),
        preferred_element_type=jnp.float32,
    )
    up_part = jnp.dot(
        tokens,
        lax.all_gather(up_pruned, "dp", axis=0, tiled=True),
        preferred_element_type=jnp.float32,
    )
    hidden = (jax.nn.silu(gate_part) * up_part).astype(jnp.bfloat16)
    down_pruned = down_weight * expand_mask(
        lax.dynamic_slice_in_dim(down_mask, row_start, row_blocks, 1)
    )
    partial_out = jnp.dot(
        hidden,
        lax.all_gather(down_pruned, "dp", axis=1, tiled=True),
        preferred_element_type=jnp.float32,
    )
    return lax.psum_scatter(
        partial_out.astype(jnp.bfloat16), "tensor", scatter_dimension=1, tiled=True
    )


def kernel(n, tok_hbm, gate_hbm, up_hbm, down_hbm, gmask_hbm, umask_hbm, dmask_hbm, out,
           gmask, umask, dmask, T, W, PC, G, psend, precv, H,
           ch_s, ch_r, ip_s, ip_r, y_s, y_r, tz_s, tz_r, tx_s, tx_r, tc_s, tc_r,
           p_s, p_r, h_s, h_r, ld):
    g = lax.axis_index("groups")
    z = lax.axis_index("dp")
    t = lax.axis_index("tensor")
    rows = tok_hbm.shape[0]
    width = gate_hbm.shape[0]
    hid = gate_hbm.shape[1]
    half = hid // 2
    quarter = rows // n
    cw = width // CHUNKS
    blocks = width // BS
    zero = jnp.int32(0)
    t_core = jnp.where(lax.rem(t, 2) == zero, t + 1, t - 1)
    t_x = lax.rem(t + 2, n)

    def mod(a):
        return lax.rem(a + 2 * n, n)

    def remote(src, dst, ss, rs, **where):
        return pltpu.make_async_remote_copy(
            src_ref=src, dst_ref=dst, send_sem=ss, recv_sem=rs, device_id=where,
            device_id_type=MESH)

    own_cols = pl.ds(pl.multiple_of(z * width, 128), width)
    load_down = pltpu.make_async_copy(
        down_hbm.at[pl.ds(pl.multiple_of(g * half, half), half), :], PC.at[z], ld.at[0])
    load_tok = pltpu.make_async_copy(
        tok_hbm.at[:, own_cols], T.at[pl.ds(pl.multiple_of(z * rows, rows), rows), :], ld.at[1])
    load_gate = pltpu.make_async_copy(gate_hbm, W.at[:, pl.ds(0, hid)], ld.at[2])
    load_up = pltpu.make_async_copy(up_hbm, W.at[:, pl.ds(hid, hid)], ld.at[3])
    load_masks = [
        pltpu.make_async_copy(src, dst, ld.at[4 + m])
        for m, (src, dst) in enumerate(
            ((dmask_hbm, dmask), (gmask_hbm, gmask), (umask_hbm, umask)))]
    load_masks[0].start()
    load_down.start()

    barrier = pltpu.get_barrier_semaphore()
    for d in range(1, n):
        pl.semaphore_signal(barrier, inc=1, device_id={"dp": mod(z + d)}, device_id_type=MESH)
        pl.semaphore_signal(barrier, inc=1, device_id={"tensor": mod(t + d)}, device_id_type=MESH)
    pl.semaphore_signal(barrier, inc=1, device_id={"groups": 1 - g}, device_id_type=MESH)
    load_masks[1].start()
    load_masks[2].start()
    load_gate.start()
    load_up.start()
    load_tok.start()

    load_masks[0].wait()
    load_down.wait()
    for b in range(blocks):
        keep = dmask[z * blocks + b].astype(jnp.float32)
        cols = pl.ds(b * BS, BS)
        PC[z, :, cols] = (PC[z, :, cols].astype(jnp.float32) * keep).astype(jnp.bfloat16)
    pl.semaphore_wait(barrier, 2 * (n - 1) + 1)

    pending = []

    def go(copy, cond=None):
        pending.append((copy, cond))
        if cond is None:
            copy.start()
        else:
            pl.when(cond)(copy.start)

    def chunk(c):
        return pl.ds(c * cw, cw)

    def g_rows(ts, h):
        return pl.ds(pl.multiple_of(ts * hid + h * half, half), half)

    def chain(direction, r, c):
        k = z - r if direction == 0 else z + r
        to = z + 1 if direction == 0 else z - 1
        ok = (k >= 0) & (to < n) if direction == 0 else (k < n) & (to >= 0)
        kk = mod(k)
        return remote(
            PC.at[kk, :, chunk(c)], PC.at[kk, :, chunk(c)], ch_s.at[direction, r, c],
            ch_r.at[direction, r, c], dp=mod(to)), ok

    def dispatch(k, slot, c, ok):
        copy = remote(
            PC.at[k, :, chunk(c)], G.at[g_rows(t, g), chunk(c)], ip_s.at[slot, c],
            ip_r.at[t, c], tensor=k)
        go(copy, ok & (k != t))

    def across(e, c):
        ts = mod(t + e)
        ref = G.at[g_rows(ts, g), chunk(c)]
        return remote(ref, ref, y_s.at[e, c], y_r.at[e, c], groups=1 - g)

    def arrived(e, c):
        ts = mod(t + e)
        ref = G.at[g_rows(ts, g), chunk(c)]
        return remote(ref, ref, ip_s.at[0, c], ip_r.at[ts, c], tensor=ts)

    crossings = [[across(e, c) for e in range(n)] for c in range(CHUNKS)]

    def owner_round(r):
        @pl.when(jnp.abs(z - t) == r)
        def _():
            for c in range(CHUNKS):
                G[g_rows(t, g), chunk(c)] = PC[t, :, chunk(c)]
                crossings[c][0].start()
                for e in range(1, n):
                    arrived(e, c).wait_recv()
                    crossings[c][e].start()

    for c in range(CHUNKS):
        for direction in range(2):
            copy, ok = chain(direction, 0, c)
            go(copy, ok)
    for c in range(CHUNKS):
        dispatch(z, 0, c, True)

    def token_piece(s, q):
        return T.at[pl.ds(pl.multiple_of(s * rows + q * quarter, quarter), quarter), :]

    for d in (2, 1, 3):
        k = mod(z + d)
        go(remote(
            tok_hbm.at[pl.ds(pl.multiple_of(t * quarter, quarter), quarter),
                       pl.ds(pl.multiple_of(k * width, 128), width)],
            token_piece(z, t), tz_s.at[d - 1], tz_r.at[d - 1], dp=k))

    def relay_tokens(d):
        s = mod(z - d)
        mine = token_piece(s, t)
        remote(mine, mine, tz_s.at[d - 1], tz_r.at[d - 1], dp=s).wait_recv()
        go(remote(mine, mine, tx_s.at[d - 1], tx_r.at[d - 1], tensor=t_x))
        go(remote(mine, mine, tc_s.at[0, d - 1], tc_r.at[0, d - 1], tensor=t_core))

    def relay_x(d):
        s = mod(z - d)
        other = token_piece(s, t_x)
        remote(other, other, tx_s.at[d - 1], tx_r.at[d - 1], tensor=t_x).wait_recv()
        go(remote(other, other, tc_s.at[1, d - 1], tc_r.at[1, d - 1], tensor=t_core))

    def products(s):
        return jnp.dot(
            T[pl.ds(pl.multiple_of(s * rows, rows), rows), :], W[...],
            preferred_element_type=jnp.float32)

    def finish_tokens(d):
        s = mod(z - d)
        for hop, q in enumerate((t_core, lax.rem(t_core + 2, n))):
            piece = token_piece(s, q)
            remote(piece, piece, tc_s.at[hop, d - 1], tc_r.at[hop, d - 1],
                   tensor=t_core).wait_recv()
        psend[d - 1] = products(s).astype(jnp.bfloat16)
        go(remote(psend.at[d - 1], precv.at[d - 1], p_s.at[d - 1], p_r.at[d - 1], dp=s))

    load_masks[1].wait()
    load_masks[2].wait()
    load_gate.wait()
    load_up.wait()

    @pl.loop(0, blocks)
    def _(b):
        at = pl.ds(pl.multiple_of(b * BS, BS), BS)
        gk = gmask[z * blocks + b].astype(jnp.float32)
        uk = umask[z * blocks + b].astype(jnp.float32)
        W[at, pl.ds(0, hid)] = (W[at, pl.ds(0, hid)].astype(jnp.float32) * gk).astype(jnp.bfloat16)
        W[at, pl.ds(hid, hid)] = (W[at, pl.ds(hid, hid)].astype(jnp.float32) * uk).astype(jnp.bfloat16)

    load_tok.wait()
    own = products(z)
    owner_round(0)

    for r in range(1, n):
        for c in range(CHUNKS):
            for direction in range(2):
                k = z - r if direction == 0 else z + r
                ok = k >= 0 if direction == 0 else k < n
                kk = mod(k)
                piece = PC.at[kk, :, chunk(c)]
                came = remote(piece, piece, ch_s.at[direction, r - 1, c],
                              ch_r.at[direction, r - 1, c], dp=mod(z + 1))
                pl.when(ok)(came.wait_recv)
                if r < n - 1:
                    copy, also = chain(direction, r, c)
                    go(copy, ok & also)
                dispatch(kk, 2 * r - 1 + direction, c, ok)
        owner_round(r)
        relay_tokens((1, 3, 2)[r - 1])
    for d in (1, 3, 2):
        relay_x(d)
    for d in (1, 3, 2):
        finish_tokens(d)

    total = own
    for d in range(1, n):
        ref = precv.at[d - 1]
        remote(ref, ref, p_s.at[d - 1], p_r.at[d - 1], dp=mod(z + d)).wait_recv()
        total = total + precv[d - 1].astype(jnp.float32)
    gate, up = total[:, :hid], total[:, hid:]
    mine = pl.ds(pl.multiple_of(t * hid, hid), hid)
    H[:, mine] = (gate / (1.0 + jnp.exp(-gate)) * up).astype(jnp.bfloat16)
    for d in range(1, n):
        go(remote(H.at[:, mine], H.at[:, mine], h_s.at[d - 1], h_r.at[d - 1], tensor=mod(t + d)))
    for d in range(1, n):
        theirs = H.at[:, pl.ds(pl.multiple_of(mod(t - d) * hid, hid), hid)]
        remote(theirs, theirs, h_s.at[d - 1], h_r.at[d - 1], tensor=mod(t + d)).wait_recv()

    for c in range(CHUNKS):
        for e in range(n):
            ts = mod(t + e)
            ref = G.at[g_rows(ts, 1 - g), chunk(c)]
            remote(ref, ref, y_s.at[e, c], y_r.at[e, c], groups=1 - g).wait_recv()
        out[:, chunk(c)] = jnp.dot(
            H[...], G[:, chunk(c)], preferred_element_type=jnp.float32).astype(jnp.bfloat16)

    for copy, cond in pending:
        if cond is None:
            copy.wait_send()
        else:
            pl.when(cond)(copy.wait_send)
    for row in crossings:
        for copy in row:
            copy.wait_send()


def fused(n, tokens, gate_weight, up_weight, down_weight, gate_mask, up_mask, down_mask):
    rows = tokens.shape[0]
    width, hid = gate_weight.shape
    bf16 = jnp.bfloat16
    dma = pltpu.SemaphoreType.DMA
    hbm = pl.BlockSpec(memory_space=pltpu.HBM)
    flags = pltpu.SMEM(gate_mask.shape[:1], jnp.int32)
    return pl.pallas_call(
        functools.partial(kernel, n),
        out_shape=jax.ShapeDtypeStruct((rows, width), bf16),
        in_specs=[hbm] * 7,
        out_specs=pl.BlockSpec(memory_space=pltpu.VMEM),
        scratch_shapes=[
            flags, flags, flags,
            pltpu.VMEM((n * rows, width), bf16),
            pltpu.VMEM((width, 2 * hid), bf16),
            pltpu.VMEM((n, hid // 2, width), bf16),
            pltpu.VMEM((n * hid, width), bf16),
            pltpu.VMEM((n - 1, rows, 2 * hid), bf16),
            pltpu.VMEM((n - 1, rows, 2 * hid), bf16),
            pltpu.VMEM((rows, n * hid), bf16),
            dma((2, n - 1, CHUNKS)), dma((2, n - 1, CHUNKS)),
            dma((2 * n - 1, CHUNKS)), dma((n, CHUNKS)),
            dma((n, CHUNKS)), dma((n, CHUNKS)),
            dma((n - 1,)), dma((n - 1,)),
            dma((n - 1,)), dma((n - 1,)),
            dma((2, n - 1)), dma((2, n - 1)),
            dma((n - 1,)), dma((n - 1,)),
            dma((n - 1,)), dma((n - 1,)),
            dma((7,)),
        ],
        compiler_params=pltpu.CompilerParams(
            collective_id=0, has_side_effects=True, vmem_limit_bytes=40 * 1024 * 1024),
        cost_estimate=pl.CostEstimate(
            flops=2 * rows * n * width * 3 * hid, bytes_accessed=16 * 1024 * 1024,
            transcendentals=rows * hid),
    )(tokens, gate_weight, up_weight, down_weight, gate_mask.reshape(-1), up_mask.reshape(-1),
      down_mask.reshape(-1))


def solution(mesh):
    n_dp, n_tensor, n_groups = mesh.shape["dp"], mesh.shape["tensor"], mesh.shape["groups"]
    placed = (
        P(("groups", "dp"), None),
        P("dp", "tensor"),
        P("dp", "tensor"),
        P("tensor", "dp"),
        P(None, "tensor"),
        P(None, "tensor"),
        P("tensor", None),
    )
    body = gathered
    if n_dp == 4 and n_tensor == 4 and n_groups == 2:
        body = functools.partial(fused, n_dp)
    return jax.shard_map(
        body, mesh=mesh, in_specs=placed, out_specs=P(("groups", "dp"), "tensor"), check_vma=False
    )
```

```python
import functools

import jax
import jax.numpy as jnp
from jax import lax
from jax.experimental import pallas as pl
from jax.experimental.pallas import tpu as pltpu
from jax.sharding import PartitionSpec as P

BS = 128
MESH = pl.DeviceIdType.MESH
CHUNKS = 2


def expand_mask(mask):
    return jnp.repeat(jnp.repeat(mask, BS, axis=0), BS, axis=1).astype(jnp.bfloat16)


def gathered(tokens, gate_weight, up_weight, down_weight, gate_mask, up_mask, down_mask):
    dp_index = lax.axis_index("dp")
    row_blocks = gate_weight.shape[0] // BS
    row_start = dp_index * row_blocks
    gate_pruned = gate_weight * expand_mask(
        lax.dynamic_slice_in_dim(gate_mask, row_start, row_blocks, 0)
    )
    up_pruned = up_weight * expand_mask(lax.dynamic_slice_in_dim(up_mask, row_start, row_blocks, 0))
    gate_part = jnp.dot(
        tokens,
        lax.all_gather(gate_pruned, "dp", axis=0, tiled=True),
        preferred_element_type=jnp.float32,
    )
    up_part = jnp.dot(
        tokens,
        lax.all_gather(up_pruned, "dp", axis=0, tiled=True),
        preferred_element_type=jnp.float32,
    )
    hidden = (jax.nn.silu(gate_part) * up_part).astype(jnp.bfloat16)
    down_pruned = down_weight * expand_mask(
        lax.dynamic_slice_in_dim(down_mask, row_start, row_blocks, 1)
    )
    partial_out = jnp.dot(
        hidden,
        lax.all_gather(down_pruned, "dp", axis=1, tiled=True),
        preferred_element_type=jnp.float32,
    )
    return lax.psum_scatter(
        partial_out.astype(jnp.bfloat16), "tensor", scatter_dimension=1, tiled=True
    )


def kernel(n, tok_hbm, gate_hbm, up_hbm, down_hbm, gmask_hbm, umask_hbm, dmask_hbm, out,
           gmask, umask, dmask, T, W, D, PC, G, psend, precv, H,
           ch_s, ch_r, ip_s, g_r, y_s, tz_s, tz_r, tx_s, tx_r, tc_s, tc_r,
           p_s, p_r, h_s, h_r, ld):
    g = lax.axis_index("groups")
    z = lax.axis_index("dp")
    t = lax.axis_index("tensor")
    rows = tok_hbm.shape[0]
    width = gate_hbm.shape[0]
    hid = gate_hbm.shape[1]
    half = hid // 2
    quarter = rows // n
    cw = width // CHUNKS
    blocks = width // BS
    zero = jnp.int32(0)
    t_core = jnp.where(lax.rem(t, 2) == zero, t + 1, t - 1)
    t_x = lax.rem(t + 2, n)

    def mod(a):
        return lax.rem(a + 2 * n, n)

    def remote(src, dst, ss, rs, **where):
        return pltpu.make_async_remote_copy(
            src_ref=src, dst_ref=dst, send_sem=ss, recv_sem=rs, device_id=where,
            device_id_type=MESH)

    own_cols = pl.ds(pl.multiple_of(z * width, 128), width)
    load_down = pltpu.make_async_copy(down_hbm, D, ld.at[0])
    load_tok = pltpu.make_async_copy(
        tok_hbm.at[:, own_cols], T.at[pl.ds(pl.multiple_of(z * rows, rows), rows), :], ld.at[1])
    load_gate = pltpu.make_async_copy(gate_hbm, W.at[:, pl.ds(0, hid)], ld.at[2])
    load_up = pltpu.make_async_copy(up_hbm, W.at[:, pl.ds(hid, hid)], ld.at[3])
    load_masks = [
        pltpu.make_async_copy(src, dst, ld.at[4 + m])
        for m, (src, dst) in enumerate(
            ((dmask_hbm, dmask), (gmask_hbm, gmask), (umask_hbm, umask)))]
    loads = [load_masks[0], load_down, load_masks[1], load_masks[2], load_gate, load_up, load_tok]
    for load in loads:
        load.start()

    barrier = pltpu.get_barrier_semaphore()
    for d in range(1, n):
        pl.semaphore_signal(barrier, inc=1, device_id={"dp": mod(z + d)}, device_id_type=MESH)
        pl.semaphore_signal(barrier, inc=1, device_id={"tensor": mod(t + d)}, device_id_type=MESH)
        pl.semaphore_signal(
            barrier, inc=1, device_id={"groups": 1 - g, "tensor": mod(t + d)}, device_id_type=MESH)
    pl.semaphore_signal(barrier, inc=1, device_id={"groups": 1 - g}, device_id_type=MESH)
    pl.semaphore_wait(barrier, 3 * (n - 1) + 1)

    pending = []

    def go(copy, cond=None):
        pending.append((copy, cond))
        if cond is None:
            copy.start()
        else:
            pl.when(cond)(copy.start)

    def chunk(c):
        return pl.ds(c * cw, cw)

    def half_rows(h):
        return pl.ds(pl.multiple_of(h * half, half), half)

    def g_rows(ts, h):
        return pl.ds(pl.multiple_of(ts * hid + h * half, half), half)

    far = jnp.where(2 * z < n, n - 1, 0)

    def side(a):
        return lax.div(a, 2)

    def relayed(src, k):
        return (side(src) != side(k)) & (k != z) & (k != far)

    def chain(direction, r, c):
        k = z - r if direction == 0 else z + r
        to = z + 1 if direction == 0 else z - 1
        ok = (k >= 0) & (to < n) if direction == 0 else (k < n) & (to >= 0)
        kk = mod(k)
        src = D.at[half_rows(g), chunk(c)] if r == 0 else PC.at[kk, :, chunk(c)]
        return remote(
            src, PC.at[kk, :, chunk(c)], ch_s.at[direction, r, c],
            ch_r.at[direction, r, c], dp=mod(to)), ok

    def dispatch(k, slot, c, ok):
        src = PC.at[k, :, chunk(c)]
        dst = G.at[g_rows(t, g), chunk(c)]
        go(remote(src, dst, ip_s.at[slot, 0, c], g_r.at[t, g, c], tensor=k), ok & (k != t))
        go(remote(src, dst, ip_s.at[slot, 1, c], g_r.at[t, g, c], groups=1 - g, tensor=k),
           ok & jnp.logical_not(relayed(t, k)))

        @pl.when(ok & (k == t))
        def _():
            G[g_rows(t, g), chunk(c)] = PC[t, :, chunk(c)]

    def arrival(ts, h, c):
        ref = G.at[g_rows(ts, h), chunk(c)]
        return remote(ref, ref, y_s.at[0, 0], g_r.at[ts, h, c], groups=1 - g)

    def across(e, c):
        ts = mod((1 - side(t)) * 2 + e)
        ref = G.at[g_rows(ts, g), chunk(c)]
        return remote(ref, ref, y_s.at[e, c], g_r.at[ts, g, c], groups=1 - g)

    crossings = [[across(e, c) for e in range(2)] for c in range(CHUNKS)]

    def owner_round(r, c):
        @pl.when((jnp.abs(z - t) == r) & (t != far))
        def _():
            for e in range(2):
                arrival(mod((1 - side(t)) * 2 + e), g, c).wait_recv()
                crossings[c][e].start()

    def token_piece(s, q):
        return T.at[pl.ds(pl.multiple_of(s * rows + q * quarter, quarter), quarter), :]

    for d in (2, 1, 3):
        k = mod(z + d)
        go(remote(
            tok_hbm.at[pl.ds(pl.multiple_of(t * quarter, quarter), quarter),
                       pl.ds(pl.multiple_of(k * width, 128), width)],
            token_piece(z, t), tz_s.at[d - 1], tz_r.at[d - 1], dp=k))

    load_masks[0].wait()
    load_down.wait()
    for b in range(blocks):
        keep = dmask[z * blocks + b].astype(jnp.float32)
        cols = pl.ds(b * BS, BS)
        D[:, cols] = (D[:, cols].astype(jnp.float32) * keep).astype(jnp.bfloat16)

    for c in range(CHUNKS):
        for direction in range(2):
            copy, ok = chain(direction, 0, c)
            go(copy, ok)
    for c in range(CHUNKS):
        for h in range(2):
            rows_h = pl.ds(h * half, half)
            go(remote(D.at[rows_h, chunk(c)], G.at[g_rows(t, h), chunk(c)],
                      ip_s.at[0, h, c], g_r.at[t, h, c], tensor=z), z != t)

    @pl.when(z == t)
    def _():
        G[pl.ds(pl.multiple_of(t * hid, hid), hid), :] = D[...]

    def relay_tokens(d):
        s = mod(z - d)
        mine = token_piece(s, t)
        remote(mine, mine, tz_s.at[d - 1], tz_r.at[d - 1], dp=s).wait_recv()
        go(remote(mine, mine, tx_s.at[d - 1], tx_r.at[d - 1], tensor=t_x))
        go(remote(mine, mine, tc_s.at[0, d - 1], tc_r.at[0, d - 1], tensor=t_core))

    def relay_x(d):
        s = mod(z - d)
        other = token_piece(s, t_x)
        remote(other, other, tx_s.at[d - 1], tx_r.at[d - 1], tensor=t_x).wait_recv()
        go(remote(other, other, tc_s.at[1, d - 1], tc_r.at[1, d - 1], tensor=t_core))

    def products(s):
        return jnp.dot(
            T[pl.ds(pl.multiple_of(s * rows, rows), rows), :], W[...],
            preferred_element_type=jnp.float32)

    def finish_tokens(d):
        s = mod(z - d)
        for hop, q in enumerate((t_core, lax.rem(t_core + 2, n))):
            piece = token_piece(s, q)
            remote(piece, piece, tc_s.at[hop, d - 1], tc_r.at[hop, d - 1],
                   tensor=t_core).wait_recv()
        psend[d - 1] = products(s).astype(jnp.bfloat16)
        go(remote(psend.at[d - 1], precv.at[d - 1], p_s.at[d - 1], p_r.at[d - 1], dp=s))

    load_masks[1].wait()
    load_masks[2].wait()
    load_gate.wait()
    load_up.wait()

    @pl.loop(0, blocks)
    def _(b):
        at = pl.ds(pl.multiple_of(b * BS, BS), BS)
        gk = gmask[z * blocks + b].astype(jnp.float32)
        uk = umask[z * blocks + b].astype(jnp.float32)
        W[at, pl.ds(0, hid)] = (W[at, pl.ds(0, hid)].astype(jnp.float32) * gk).astype(jnp.bfloat16)
        W[at, pl.ds(hid, hid)] = (W[at, pl.ds(hid, hid)].astype(jnp.float32) * uk).astype(jnp.bfloat16)

    load_tok.wait()
    own = products(z)

    def chain_step(r, c):
        for direction in range(2):
            k = z - r if direction == 0 else z + r
            ok = k >= 0 if direction == 0 else k < n
            kk = mod(k)
            piece = PC.at[kk, :, chunk(c)]
            came = remote(piece, piece, ch_s.at[direction, r - 1, c],
                          ch_r.at[direction, r - 1, c], dp=mod(z + 1))
            pl.when(ok)(came.wait_recv)
            if r < n - 1:
                copy, also = chain(direction, r, c)
                go(copy, ok & also)
            dispatch(kk, 2 * r - 1 + direction, c, ok)
        if r < n - 1 and c > 0:
            owner_round(r, c - 1)

    def chain_round(r):
        for c in range(CHUNKS):
            chain_step(r, c)

    relay_tokens(1)
    relay_tokens(3)
    chain_round(1)
    relay_tokens(2)
    relay_x(1)
    relay_x(3)
    owner_round(1, CHUNKS - 1)
    chain_round(2)
    relay_x(2)
    owner_round(2, CHUNKS - 1)
    finish_tokens(1)
    finish_tokens(3)
    finish_tokens(2)
    chain_round(3)

    total = own
    for d in range(1, n):
        ref = precv.at[d - 1]
        remote(ref, ref, p_s.at[d - 1], p_r.at[d - 1], dp=mod(z + d)).wait_recv()
        total = total + precv[d - 1].astype(jnp.float32)
    gate, up = total[:, :hid], total[:, hid:]
    mine = pl.ds(pl.multiple_of(t * hid, hid), hid)
    H[:, mine] = (gate / (1.0 + jnp.exp(-gate)) * up).astype(jnp.bfloat16)
    for d in range(1, n):
        go(remote(H.at[:, mine], H.at[:, mine], h_s.at[d - 1], h_r.at[d - 1], tensor=mod(t + d)))
    for d in range(1, n):
        theirs = H.at[:, pl.ds(pl.multiple_of(mod(t - d) * hid, hid), hid)]
        remote(theirs, theirs, h_s.at[d - 1], h_r.at[d - 1], tensor=mod(t + d)).wait_recv()

    for c in range(CHUNKS):
        for ts in range(n):
            for h in range(2):
                held = (t == ts) & ((z == t) | (g == h))
                passed = (g == h) & relayed(ts, t)
                pl.when(jnp.logical_not(held | passed))(arrival(jnp.int32(ts), jnp.int32(h), c).wait_recv)
        out[:, chunk(c)] = jnp.dot(
            H[...], G[:, chunk(c)], preferred_element_type=jnp.float32).astype(jnp.bfloat16)

    for copy, cond in pending:
        if cond is None:
            copy.wait_send()
        else:
            pl.when(cond)(copy.wait_send)

    @pl.when((z != t) & (t != far))
    def _():
        for row in crossings:
            for copy in row:
                copy.wait_send()


def fused(n, tokens, gate_weight, up_weight, down_weight, gate_mask, up_mask, down_mask):
    rows = tokens.shape[0]
    width, hid = gate_weight.shape
    bf16 = jnp.bfloat16
    dma = pltpu.SemaphoreType.DMA
    hbm = pl.BlockSpec(memory_space=pltpu.HBM)
    flags = pltpu.SMEM(gate_mask.shape[:1], jnp.int32)
    return pl.pallas_call(
        functools.partial(kernel, n),
        out_shape=jax.ShapeDtypeStruct((rows, width), bf16),
        in_specs=[hbm] * 7,
        out_specs=pl.BlockSpec(memory_space=pltpu.VMEM),
        scratch_shapes=[
            flags, flags, flags,
            pltpu.VMEM((n * rows, width), bf16),
            pltpu.VMEM((width, 2 * hid), bf16),
            pltpu.VMEM((hid, width), bf16),
            pltpu.VMEM((n, hid // 2, width), bf16),
            pltpu.VMEM((n * hid, width), bf16),
            pltpu.VMEM((n - 1, rows, 2 * hid), bf16),
            pltpu.VMEM((n - 1, rows, 2 * hid), bf16),
            pltpu.VMEM((rows, n * hid), bf16),
            dma((2, n - 1, CHUNKS)), dma((2, n - 1, CHUNKS)),
            dma((2 * n - 1, 2, CHUNKS)), dma((n, 2, CHUNKS)),
            dma((2, CHUNKS)),
            dma((n - 1,)), dma((n - 1,)),
            dma((n - 1,)), dma((n - 1,)),
            dma((2, n - 1)), dma((2, n - 1)),
            dma((n - 1,)), dma((n - 1,)),
            dma((n - 1,)), dma((n - 1,)),
            dma((7,)),
        ],
        compiler_params=pltpu.CompilerParams(
            collective_id=0, has_side_effects=True, vmem_limit_bytes=63 * 1024 * 1024),
        cost_estimate=pl.CostEstimate(
            flops=2 * rows * n * width * 3 * hid, bytes_accessed=16 * 1024 * 1024,
            transcendentals=rows * hid),
    )(tokens, gate_weight, up_weight, down_weight, gate_mask.reshape(-1), up_mask.reshape(-1),
      down_mask.reshape(-1))


def solution(mesh):
    n_dp, n_tensor, n_groups = mesh.shape["dp"], mesh.shape["tensor"], mesh.shape["groups"]
    placed = (
        P(("groups", "dp"), None),
        P("dp", "tensor"),
        P("dp", "tensor"),
        P("tensor", "dp"),
        P(None, "tensor"),
        P(None, "tensor"),
        P("tensor", None),
    )
    body = gathered
    if n_dp == 4 and n_tensor == 4 and n_groups == 2:
        body = functools.partial(fused, n_dp)
    return jax.shard_map(
        body, mesh=mesh, in_specs=placed, out_specs=P(("groups", "dp"), "tensor"), check_vma=False
    )
```

```python
import functools

import jax
import jax.numpy as jnp
from jax import lax
from jax.experimental import pallas as pl
from jax.experimental.pallas import tpu as pltpu
from jax.sharding import PartitionSpec as P

BS = 128
MESH = pl.DeviceIdType.MESH
CHUNKS = 2


def expand_mask(mask):
    return jnp.repeat(jnp.repeat(mask, BS, axis=0), BS, axis=1).astype(jnp.bfloat16)


def gathered(tokens, gate_weight, up_weight, down_weight, gate_mask, up_mask, down_mask):
    dp_index = lax.axis_index("dp")
    row_blocks = gate_weight.shape[0] // BS
    row_start = dp_index * row_blocks
    gate_pruned = gate_weight * expand_mask(
        lax.dynamic_slice_in_dim(gate_mask, row_start, row_blocks, 0)
    )
    up_pruned = up_weight * expand_mask(lax.dynamic_slice_in_dim(up_mask, row_start, row_blocks, 0))
    gate_part = jnp.dot(
        tokens,
        lax.all_gather(gate_pruned, "dp", axis=0, tiled=True),
        preferred_element_type=jnp.float32,
    )
    up_part = jnp.dot(
        tokens,
        lax.all_gather(up_pruned, "dp", axis=0, tiled=True),
        preferred_element_type=jnp.float32,
    )
    hidden = (jax.nn.silu(gate_part) * up_part).astype(jnp.bfloat16)
    down_pruned = down_weight * expand_mask(
        lax.dynamic_slice_in_dim(down_mask, row_start, row_blocks, 1)
    )
    partial_out = jnp.dot(
        hidden,
        lax.all_gather(down_pruned, "dp", axis=1, tiled=True),
        preferred_element_type=jnp.float32,
    )
    return lax.psum_scatter(
        partial_out.astype(jnp.bfloat16), "tensor", scatter_dimension=1, tiled=True
    )


def kernel(n, tok_hbm, gate_hbm, up_hbm, down_hbm, gmask_hbm, umask_hbm, dmask_hbm, out,
           gmask, umask, dmask, T, W, D, PC, G, psend, precv, H,
           ch_s, ch_r, ip_s, g_r, y_s, tz_s, tz_r, tx_s, tx_r, tc_s, tc_r,
           p_s, p_r, h_s, h_r, ld):
    g = lax.axis_index("groups")
    z = lax.axis_index("dp")
    t = lax.axis_index("tensor")
    rows = tok_hbm.shape[0]
    width = gate_hbm.shape[0]
    hid = gate_hbm.shape[1]
    half = hid // 2
    quarter = rows // n
    cw = width // CHUNKS
    blocks = width // BS
    zero = jnp.int32(0)
    t_core = jnp.where(lax.rem(t, 2) == zero, t + 1, t - 1)
    t_x = lax.rem(t + 2, n)

    def mod(a):
        return lax.rem(a + 2 * n, n)

    def remote(src, dst, ss, rs, **where):
        return pltpu.make_async_remote_copy(
            src_ref=src, dst_ref=dst, send_sem=ss, recv_sem=rs, device_id=where,
            device_id_type=MESH)

    own_cols = pl.ds(pl.multiple_of(z * width, 128), width)
    load_down = pltpu.make_async_copy(down_hbm, D, ld.at[0])
    load_tok = pltpu.make_async_copy(
        tok_hbm.at[:, own_cols], T.at[pl.ds(pl.multiple_of(z * rows, rows), rows), :], ld.at[1])
    load_gate = pltpu.make_async_copy(gate_hbm, W.at[:, pl.ds(0, hid)], ld.at[2])
    load_up = pltpu.make_async_copy(up_hbm, W.at[:, pl.ds(hid, hid)], ld.at[3])
    load_masks = [
        pltpu.make_async_copy(src, dst, ld.at[4 + m])
        for m, (src, dst) in enumerate(
            ((dmask_hbm, dmask), (gmask_hbm, gmask), (umask_hbm, umask)))]
    loads = [load_masks[0], load_down, load_masks[1], load_masks[2], load_gate, load_up, load_tok]
    for load in loads:
        load.start()

    barrier = pltpu.get_barrier_semaphore()
    for d in range(1, n):
        pl.semaphore_signal(barrier, inc=1, device_id={"dp": mod(z + d)}, device_id_type=MESH)
        pl.semaphore_signal(barrier, inc=1, device_id={"tensor": mod(t + d)}, device_id_type=MESH)
        pl.semaphore_signal(
            barrier, inc=1, device_id={"groups": 1 - g, "tensor": mod(t + d)}, device_id_type=MESH)
    pl.semaphore_signal(barrier, inc=1, device_id={"groups": 1 - g}, device_id_type=MESH)
    pl.semaphore_wait(barrier, 3 * (n - 1) + 1)

    pending = []

    def go(copy, cond=None):
        pending.append((copy, cond))
        if cond is None:
            copy.start()
        else:
            pl.when(cond)(copy.start)

    def chunk(c):
        return pl.ds(c * cw, cw)

    def half_rows(h):
        return pl.ds(pl.multiple_of(h * half, half), half)

    def g_rows(ts, h):
        return pl.ds(pl.multiple_of(ts * hid + h * half, half), half)

    far = jnp.where(2 * z < n, n - 1, 0)

    def side(a):
        return lax.div(a, 2)

    def relayed(src, k):
        return (side(src) != side(k)) & (k != z) & (k != far)

    def chain(direction, r, c):
        k = z - r if direction == 0 else z + r
        to = z + 1 if direction == 0 else z - 1
        ok = (k >= 0) & (to < n) if direction == 0 else (k < n) & (to >= 0)
        kk = mod(k)
        src = D.at[half_rows(g), chunk(c)] if r == 0 else PC.at[kk, :, chunk(c)]
        return remote(
            src, PC.at[kk, :, chunk(c)], ch_s.at[direction, r, c],
            ch_r.at[direction, r, c], dp=mod(to)), ok

    def dispatch(k, slot, c, ok):
        src = PC.at[k, :, chunk(c)]
        dst = G.at[g_rows(t, g), chunk(c)]
        go(remote(src, dst, ip_s.at[slot, 0, c], g_r.at[t, g, c], tensor=k), ok & (k != t))
        go(remote(src, dst, ip_s.at[slot, 1, c], g_r.at[t, g, c], groups=1 - g, tensor=k),
           ok & jnp.logical_not(relayed(t, k)))

        @pl.when(ok & (k == t))
        def _():
            G[g_rows(t, g), chunk(c)] = PC[t, :, chunk(c)]

    def arrival(ts, h, c):
        ref = G.at[g_rows(ts, h), chunk(c)]
        return remote(ref, ref, y_s.at[0, 0], g_r.at[ts, h, c], groups=1 - g)

    def across(e, c):
        ts = mod((1 - side(t)) * 2 + e)
        ref = G.at[g_rows(ts, g), chunk(c)]
        return remote(ref, ref, y_s.at[e, c], g_r.at[ts, g, c], groups=1 - g)

    crossings = [[across(e, c) for e in range(2)] for c in range(CHUNKS)]

    def owner_round(r, c):
        @pl.when((jnp.abs(z - t) == r) & (t != far))
        def _():
            for e in range(2):
                arrival(mod((1 - side(t)) * 2 + e), g, c).wait_recv()
                crossings[c][e].start()

    def token_piece(s, q):
        return T.at[pl.ds(pl.multiple_of(s * rows + q * quarter, quarter), quarter), :]

    for d in (2, 1, 3):
        k = mod(z + d)
        go(remote(
            tok_hbm.at[pl.ds(pl.multiple_of(t * quarter, quarter), quarter),
                       pl.ds(pl.multiple_of(k * width, 128), width)],
            token_piece(z, t), tz_s.at[d - 1], tz_r.at[d - 1], dp=k))

    load_masks[0].wait()
    load_down.wait()
    for b in range(blocks):
        keep = dmask[z * blocks + b].astype(jnp.float32)
        cols = pl.ds(b * BS, BS)
        D[:, cols] = (D[:, cols].astype(jnp.float32) * keep).astype(jnp.bfloat16)

    for c in range(CHUNKS):
        for direction in range(2):
            copy, ok = chain(direction, 0, c)
            go(copy, ok)
    @pl.when(z == t)
    def _():
        G[pl.ds(pl.multiple_of(t * hid, hid), hid), :] = D[...]

    def relay_tokens(d):
        s = mod(z - d)
        mine = token_piece(s, t)
        remote(mine, mine, tz_s.at[d - 1], tz_r.at[d - 1], dp=s).wait_recv()
        go(remote(mine, mine, tx_s.at[d - 1], tx_r.at[d - 1], tensor=t_x))
        go(remote(mine, mine, tc_s.at[0, d - 1], tc_r.at[0, d - 1], tensor=t_core))

    def relay_x(d):
        s = mod(z - d)
        other = token_piece(s, t_x)
        remote(other, other, tx_s.at[d - 1], tx_r.at[d - 1], tensor=t_x).wait_recv()
        go(remote(other, other, tc_s.at[1, d - 1], tc_r.at[1, d - 1], tensor=t_core))

    def products(s):
        return jnp.dot(
            T[pl.ds(pl.multiple_of(s * rows, rows), rows), :], W[...],
            preferred_element_type=jnp.float32)

    def finish_tokens(d):
        s = mod(z - d)
        for hop, q in enumerate((t_core, lax.rem(t_core + 2, n))):
            piece = token_piece(s, q)
            remote(piece, piece, tc_s.at[hop, d - 1], tc_r.at[hop, d - 1],
                   tensor=t_core).wait_recv()
        psend[d - 1] = products(s).astype(jnp.bfloat16)
        go(remote(psend.at[d - 1], precv.at[d - 1], p_s.at[d - 1], p_r.at[d - 1], dp=s))

    load_masks[1].wait()
    load_masks[2].wait()
    load_gate.wait()
    load_up.wait()

    @pl.loop(0, blocks)
    def _(b):
        at = pl.ds(pl.multiple_of(b * BS, BS), BS)
        gk = gmask[z * blocks + b].astype(jnp.float32)
        uk = umask[z * blocks + b].astype(jnp.float32)
        W[at, pl.ds(0, hid)] = (W[at, pl.ds(0, hid)].astype(jnp.float32) * gk).astype(jnp.bfloat16)
        W[at, pl.ds(hid, hid)] = (W[at, pl.ds(hid, hid)].astype(jnp.float32) * uk).astype(jnp.bfloat16)

    load_tok.wait()
    own = products(z)

    def chain_step(r, c):
        for direction in range(2):
            k = z - r if direction == 0 else z + r
            ok = k >= 0 if direction == 0 else k < n
            kk = mod(k)
            piece = PC.at[kk, :, chunk(c)]
            came = remote(piece, piece, ch_s.at[direction, r - 1, c],
                          ch_r.at[direction, r - 1, c], dp=mod(z + 1))
            pl.when(ok)(came.wait_recv)
            if r < n - 1:
                copy, also = chain(direction, r, c)
                go(copy, ok & also)
            dispatch(kk, 2 * r - 1 + direction, c, ok)
        if r < n - 1 and c > 0:
            owner_round(r, c - 1)

    def chain_round(r):
        for c in range(CHUNKS):
            chain_step(r, c)

    relay_tokens(1)
    relay_tokens(3)
    chain_round(1)
    relay_tokens(2)
    relay_x(1)
    relay_x(3)
    owner_round(1, CHUNKS - 1)
    chain_round(2)
    relay_x(2)
    owner_round(2, CHUNKS - 1)
    for c in range(CHUNKS):
        for h in range(2):
            rows_h = pl.ds(h * half, half)
            go(remote(D.at[rows_h, chunk(c)], G.at[g_rows(t, h), chunk(c)],
                      ip_s.at[0, h, c], g_r.at[t, h, c], tensor=z), z != t)

    finish_tokens(1)
    finish_tokens(3)
    finish_tokens(2)
    chain_round(3)

    total = own
    for d in range(1, n):
        ref = precv.at[d - 1]
        remote(ref, ref, p_s.at[d - 1], p_r.at[d - 1], dp=mod(z + d)).wait_recv()
        total = total + precv[d - 1].astype(jnp.float32)
    gate, up = total[:, :hid], total[:, hid:]
    mine = pl.ds(pl.multiple_of(t * hid, hid), hid)
    H[:, mine] = (gate / (1.0 + jnp.exp(-gate)) * up).astype(jnp.bfloat16)
    for d in range(1, n):
        go(remote(H.at[:, mine], H.at[:, mine], h_s.at[d - 1], h_r.at[d - 1], tensor=mod(t + d)))
    for d in range(1, n):
        theirs = H.at[:, pl.ds(pl.multiple_of(mod(t - d) * hid, hid), hid)]
        remote(theirs, theirs, h_s.at[d - 1], h_r.at[d - 1], tensor=mod(t + d)).wait_recv()

    for c in range(CHUNKS):
        for ts in range(n):
            for h in range(2):
                held = (t == ts) & ((z == t) | (g == h))
                passed = (g == h) & relayed(ts, t)
                pl.when(jnp.logical_not(held | passed))(arrival(jnp.int32(ts), jnp.int32(h), c).wait_recv)
        out[:, chunk(c)] = jnp.dot(
            H[...], G[:, chunk(c)], preferred_element_type=jnp.float32).astype(jnp.bfloat16)

    for copy, cond in pending:
        if cond is None:
            copy.wait_send()
        else:
            pl.when(cond)(copy.wait_send)

    @pl.when((z != t) & (t != far))
    def _():
        for row in crossings:
            for copy in row:
                copy.wait_send()


def fused(n, tokens, gate_weight, up_weight, down_weight, gate_mask, up_mask, down_mask):
    rows = tokens.shape[0]
    width, hid = gate_weight.shape
    bf16 = jnp.bfloat16
    dma = pltpu.SemaphoreType.DMA
    hbm = pl.BlockSpec(memory_space=pltpu.HBM)
    flags = pltpu.SMEM(gate_mask.shape[:1], jnp.int32)
    return pl.pallas_call(
        functools.partial(kernel, n),
        out_shape=jax.ShapeDtypeStruct((rows, width), bf16),
        in_specs=[hbm] * 7,
        out_specs=pl.BlockSpec(memory_space=pltpu.VMEM),
        scratch_shapes=[
            flags, flags, flags,
            pltpu.VMEM((n * rows, width), bf16),
            pltpu.VMEM((width, 2 * hid), bf16),
            pltpu.VMEM((hid, width), bf16),
            pltpu.VMEM((n, hid // 2, width), bf16),
            pltpu.VMEM((n * hid, width), bf16),
            pltpu.VMEM((n - 1, rows, 2 * hid), bf16),
            pltpu.VMEM((n - 1, rows, 2 * hid), bf16),
            pltpu.VMEM((rows, n * hid), bf16),
            dma((2, n - 1, CHUNKS)), dma((2, n - 1, CHUNKS)),
            dma((2 * n - 1, 2, CHUNKS)), dma((n, 2, CHUNKS)),
            dma((2, CHUNKS)),
            dma((n - 1,)), dma((n - 1,)),
            dma((n - 1,)), dma((n - 1,)),
            dma((2, n - 1)), dma((2, n - 1)),
            dma((n - 1,)), dma((n - 1,)),
            dma((n - 1,)), dma((n - 1,)),
            dma((7,)),
        ],
        compiler_params=pltpu.CompilerParams(
            collective_id=0, has_side_effects=True, vmem_limit_bytes=63 * 1024 * 1024),
        cost_estimate=pl.CostEstimate(
            flops=2 * rows * n * width * 3 * hid, bytes_accessed=16 * 1024 * 1024,
            transcendentals=rows * hid),
    )(tokens, gate_weight, up_weight, down_weight, gate_mask.reshape(-1), up_mask.reshape(-1),
      down_mask.reshape(-1))


def solution(mesh):
    n_dp, n_tensor, n_groups = mesh.shape["dp"], mesh.shape["tensor"], mesh.shape["groups"]
    placed = (
        P(("groups", "dp"), None),
        P("dp", "tensor"),
        P("dp", "tensor"),
        P("tensor", "dp"),
        P(None, "tensor"),
        P(None, "tensor"),
        P("tensor", None),
    )
    body = gathered
    if n_dp == 4 and n_tensor == 4 and n_groups == 2:
        body = functools.partial(fused, n_dp)
    return jax.shard_map(
        body, mesh=mesh, in_specs=placed, out_specs=P(("groups", "dp"), "tensor"), check_vma=False
    )
```
